32 devices in a mesh: groups: 2 (over x), shard: 16 (over z, y, core).
Axes of the slice: x: 2, y: 2, z: 4, core: 2. Of those that a mesh axis runs over, the one named last changes fastest.
Arguments:
- embed: bfloat16 [65536, 768], P(('groups', 'shard')), parts along dimension 0, may hold values from -6 to 6
- seed_mask: int32 [65536], P(('groups', 'shard')), parts along dimension 0, may hold values 0 or 1
- seed_class: int32 [65536], P(('groups', 'shard')), parts along dimension 0, may hold values from 0 to 255
- partner: int32 [32, 16], P(('groups', 'shard')), parts along dimension 0, may hold values from 0 to 7
- pair_local: int32 [2048], P(('groups', 'shard')), parts along dimension 0, may hold values from 0 to 7, as said below
- pair_peer: int32 [2048], P(('groups', 'shard')), parts along dimension 0, may hold values from 0 to 15, as said below
Outputs:
- labels: float32 [65536, 256], P(('groups', 'shard')), parts along dimension 0
The draws below stay inside these ranges and needn't reach their ends.
There are 2 independent parts, one for each index of `groups`. The reference program is written for one: setup_inputs(seed, part) draws one part's arguments, and reference() takes and returns one part's arrays. A program takes and returns all parts, laid end to end along the dimension named above; each array names one. Nothing has to cross between parts.
Inputs may be any that keep to these rules, and one draw needn't show every extreme that they name: `pair_peer`: row r belongs to device r // 64 of shard, and its partner device is never that device itself; each device has pairs with the device after it and with the device before it, counted round. No two pairs of one device have both the same pair_local and the same pair_peer.
All inputs are finite; a program needn't handle non-finite values. No bound on the sum of `seed_mask` on one device may be relied on, other than what follows from the above.
Results may differ from the reference program's by a relative error of at most 0.0011.
Values may be sent and summed in bfloat16 or wider, within the bound.
No kernel may reach another device: no remote copies, remote signals or barrier semaphores. Data moves between devices by JAX's collectives and lax.ppermute only.
A program may use at most 128 MiB of HBM per device.

```python
import jax
import jax.numpy as jnp
from jax import lax

D = 768
C = 256
TILE = 256
TILES_PER_DEVICE = 8
PAIRS_DEV = 64
ITERS = 2
ROWS = 32768
N_SHARD = 16


center_spread = 1.5


noise_spread = 0.5


def pair_choice(key):
    tile_combinations = TILES_PER_DEVICE * (N_SHARD - 1)

    def device_share(device):
        sub = jax.random.fold_in(key, device)
        sorted_key_list, ranking_key_score = jax.random.split(sub)
        order = jax.random.permutation(sorted_key_list, TILES_PER_DEVICE).astype(jnp.int32)
        tile_combination = jnp.arange(tile_combinations, dtype=jnp.int32)
        rank = tile_combination % TILES_PER_DEVICE
        offset = 1 + tile_combination // TILES_PER_DEVICE
        edge_weight = TILES_PER_DEVICE // (rank + 1) * (N_SHARD // offset)
        mandatory_pick = ((rank == 0) & ((offset == 1) | (offset == N_SHARD - 1))).astype(jnp.int32)
        extra_reward = mandatory_pick * (1024 * TILES_PER_DEVICE * N_SHARD * tile_combinations)
        pair_rating = jax.random.randint(ranking_key_score, (tile_combinations,), 1, 1024) * edge_weight * tile_combinations + tile_combination + extra_reward
        unused, chosen = lax.top_k(pair_rating, PAIRS_DEV)
        chosen = chosen.astype(jnp.int32)
        local = order[chosen % TILES_PER_DEVICE]
        peer = (device + 1 + chosen // TILES_PER_DEVICE) % N_SHARD
        return (local.astype(jnp.int32), peer.astype(jnp.int32))
    local, peer = jax.vmap(device_share)(jnp.arange(N_SHARD, dtype=jnp.int32))
    return (local.reshape(-1), peer.reshape(-1))


def cluster_index(key):
    return jax.random.randint(jax.random.fold_in(key, 41), (ROWS,), 0, C // 4).astype(jnp.int32)


def draw_pair_local(key, part):
    return pair_choice(jax.random.fold_in(key, 21))[0]


def draw_pair_peer(key, part):
    return pair_choice(jax.random.fold_in(key, 21))[1]


def draw_embed(key, part):
    cluster = cluster_index(key)
    key = jax.random.fold_in(key, 42)
    center_key, noise_key = jax.random.split(key, 2)
    centers = jax.random.normal(center_key, (C // 4, D), jnp.float32) * center_spread
    noise = jax.random.normal(noise_key, (ROWS, D), jnp.float32) * noise_spread
    values = jnp.clip(centers[cluster] + noise, -6.0, 6.0)
    return values.astype(jnp.bfloat16)


def draw_seed_class(key, part):
    cluster = cluster_index(key)
    key = jax.random.fold_in(key, 43)
    within = jax.random.randint(key, (ROWS,), 0, 4).astype(jnp.int32)
    return (4 * cluster + within).astype(jnp.int32)


def set_ends(result, stream_key, low, largest):
    longest = result.shape.index(max(result.shape))
    spots = []
    for shift in (0, 1):
        where = [jax.random.randint(jax.random.fold_in(stream_key, axis), (), 0, length) for axis, length in enumerate(result.shape)]
        where[longest] = (where[longest] + shift) % result.shape[longest]
        spots.append(tuple(where))
    return result.at[spots[0]].set(low).at[spots[1]].set(largest)


def setup_inputs(seed: int = 0, part: int = 0) -> dict:
    arg_keys = jax.random.split(jax.random.key(seed), 7)
    part_keys = jax.random.split(jax.random.fold_in(arg_keys[6], part), 7)
    return {
        "embed": draw_embed(jax.random.fold_in(jax.random.fold_in(arg_keys[6], part), 71), part),
        "seed_mask": set_ends((jax.random.randint(part_keys[1], (ROWS,), 0, 4) < 1).astype(jnp.int32), jax.random.fold_in(part_keys[1], 1), 0, 1),
        "seed_class": draw_seed_class(jax.random.fold_in(jax.random.fold_in(arg_keys[6], part), 71), part),
        "partner": set_ends(jax.random.randint(part_keys[3], (N_SHARD, N_SHARD), 0, TILES_PER_DEVICE), jax.random.fold_in(part_keys[3], 1), 0, TILES_PER_DEVICE - 1).astype(jnp.int32),
        "pair_local": draw_pair_local(jax.random.fold_in(jax.random.fold_in(arg_keys[6], part), 71), part),
        "pair_peer": draw_pair_peer(jax.random.fold_in(jax.random.fold_in(arg_keys[6], part), 71), part),
    }


sharpness = 1.0
mixing = 0.8


def reference(embed, seed_mask, seed_class, partner, pair_local, pair_peer):
    tile_data = embed.reshape(-1, TILE, D)
    tile_count = tile_data.shape[0]
    row_norms = jnp.sum(jnp.square(embed.astype(jnp.float32)), axis=1).reshape(-1, TILE)
    pair_total = pair_local.shape[0]
    planned = (jnp.arange(pair_total) // PAIRS_DEV).astype(jnp.int32)
    first_tile = (planned * TILES_PER_DEVICE + pair_local).astype(jnp.int32)
    second_tile = (pair_peer * TILES_PER_DEVICE + partner[pair_peer, planned]).astype(jnp.int32)

    def pair_kernel(index):
        first = first_tile[index]
        second = second_tile[index]
        left = tile_data[first].astype(jnp.float32)
        right = tile_data[second].astype(jnp.float32)
        inner = jnp.dot(left, right.T, precision=lax.Precision.HIGHEST)
        exponent = (2.0 * D - row_norms[first][:, None] - row_norms[second][None, :] + 2.0 * inner) * (sharpness / D)
        return jnp.exp(exponent).astype(jnp.bfloat16)

    kernel_matrices = lax.map(pair_kernel, jnp.arange(pair_total))
    degree = jnp.ones((tile_count, TILE), jnp.float32)
    degree = degree.at[first_tile].add(jnp.sum(kernel_matrices.astype(jnp.float32), axis=2))
    degree = degree.at[second_tile].add(jnp.sum(kernel_matrices.astype(jnp.float32), axis=1))
    classes = jnp.arange(C)
    seeded = (seed_mask == 1)[:, None]
    target = jnp.where(seeded & (seed_class[:, None] == classes[None, :]), 1.0, 0.0).astype(jnp.float32)
    labels = jnp.where(seeded, target, 1.0 / C).astype(jnp.float32)
    for sweep in range(ITERS):
        rounded = labels.astype(jnp.bfloat16).reshape(tile_count, TILE, C)

        def add_pair(running, index):
            kernel = kernel_matrices[index].astype(jnp.float32)
            first = first_tile[index]
            second = second_tile[index]
            gathered_labels = jnp.dot(kernel, rounded[second].astype(jnp.float32), precision=lax.Precision.HIGHEST)
            pushed = jnp.dot(kernel.T, rounded[first].astype(jnp.float32), precision=lax.Precision.HIGHEST)
            running = running.at[first].add(gathered_labels).at[second].add(pushed)
            return running, None

        summed, unused = lax.scan(add_pair, jnp.zeros((tile_count, TILE, C), jnp.float32), jnp.arange(pair_total))
        averaged = (labels + summed.reshape(-1, C)) / degree.reshape(-1)[:, None]
        blended = mixing * averaged + (1.0 - mixing) * target
        squared = blended * blended
        labels = squared / jnp.sum(squared, axis=1, keepdims=True)
    return labels
```

```python
import math

import jax
import jax.numpy as jnp
from jax import lax
from jax.experimental import pallas as pl
from jax.experimental.pallas import tpu as pltpu
from jax.sharding import PartitionSpec as P

C = 256
TILE = 256
ITERS = 2
WINDOW = 4

sharpness = 1.0
mixing = 0.8

LOG2E = math.log2(math.e)


def slot_kernel(sel, eloc, erem, bloc, brem, lloc, lrem, gin, kout, pout, gout, *, scale):
    step = pl.program_id(0)
    count = sel[0]

    @pl.when(step == 0)
    def _():
        pout[...] = jnp.zeros_like(pout)

    @pl.when((step == 0) & (count == 0))
    def _():
        gout[...] = gin[...]
        kout[...] = jnp.zeros_like(kout)

    @pl.when(step < count)
    def _():
        inner = lax.dot_general(
            eloc[0], erem[...], (((1,), (1,)), ((), ())), preferred_element_type=jnp.float32
        )
        k = jnp.exp2(inner * scale + (bloc[0] + brem[...])).astype(jnp.bfloat16)
        kout[0] = k
        gout[0] = gin[0] + jnp.dot(k, lrem[...], preferred_element_type=jnp.float32)
        pout[...] += lax.dot_general(
            k, lloc[0], (((0,), (0,)), ((), ())), preferred_element_type=jnp.float32
        )


def push_kernel(sel, kref, lloc, pout):
    step = pl.program_id(0)

    @pl.when(step == 0)
    def _():
        pout[...] = jnp.zeros_like(pout)

    @pl.when(step < sel[0])
    def _():
        pout[...] += lax.dot_general(
            kref[0], lloc[0], (((0,), (0,)), ((), ())), preferred_element_type=jnp.float32
        )


def gather_kernel(sel, kref, lrem, gin, gout):
    step = pl.program_id(0)
    count = sel[0]

    @pl.when((step == 0) & (count == 0))
    def _():
        gout[...] = gin[...]

    @pl.when(step < count)
    def _():
        gout[0] = gin[0] + jnp.dot(kref[0], lrem[...], preferred_element_type=jnp.float32)


def body(embed, seed_mask, seed_class, partner, pair_local, pair_peer):
    n = lax.axis_size("shard")
    me = lax.axis_index("shard")
    features = embed.shape[1]
    tiles = embed.reshape(-1, TILE, features)
    count_t = tiles.shape[0]
    mine = partner.reshape(-1)
    half = n // 2
    order = []
    for k in range(half):
        order.append(half + k)
        if k + 1 < half:
            order.append(k + 1)

    def swap(value, s):
        return lax.ppermute(value, "shard", [(q, q ^ s) for q in range(n)])

    tile_ids = jnp.arange(count_t, dtype=jnp.int32)
    shard_ids = jnp.arange(n, dtype=jnp.int32)
    active = jnp.any(
        (pair_peer[None, None, :] == shard_ids[:, None, None])
        & (pair_local[None, None, :] == tile_ids[None, :, None]),
        axis=2,
    )
    counts = jnp.sum(active.astype(jnp.int32), axis=1)
    place = jnp.sum(
        (active[:, None, :] & (tile_ids[None, None, :] < tile_ids[None, :, None])).astype(jnp.int32), axis=2
    )
    wanted = jnp.minimum(tile_ids[None, :], jnp.maximum(counts - 1, 0)[:, None])
    listed = jnp.sum(
        jnp.where(active[:, None, :] & (place[:, None, :] == wanted[:, :, None]), tile_ids[None, None, :], 0),
        axis=2,
    )
    selection = jnp.concatenate([counts[:, None], listed], axis=1).astype(jnp.int32)

    norms = jnp.sum(jnp.square(tiles.astype(jnp.float32)), axis=2)
    bias = (1.0 - norms * (1.0 / features)) * (sharpness * LOG2E)
    seeded = seed_mask == 1
    classes = jnp.where(seeded, seed_class, -1).reshape(count_t, TILE)
    meta = jnp.stack([bias, classes.astype(jnp.float32)], axis=1)
    meta_in = lax.all_to_all(meta[mine], "shard", split_axis=0, concat_axis=0, tiled=True)
    class_ids = jnp.arange(C, dtype=jnp.float32)

    def first_labels(ids):
        return jnp.where(
            ids[..., None] < 0, 1.0 / C, (ids[..., None] == class_ids).astype(jnp.float32)
        )

    labels = first_labels(classes.astype(jnp.float32))
    target = jnp.where(seeded.reshape(count_t, TILE)[..., None], labels, 0.0)
    rounded = labels.astype(jnp.bfloat16)
    rounded_in = first_labels(meta_in[:, 1]).astype(jnp.bfloat16)
    bias_column = bias[:, :, None]

    block = (1, TILE, C)

    def at_list(g, sel):
        return (sel[1 + g], 0, 0)

    def at_place(g, sel):
        return (jnp.minimum(g, jnp.maximum(sel[0] - 1, 0)), 0, 0)

    def whole(g, sel):
        return (0, 0)

    estimate = pl.CostEstimate(flops=int(2e9), bytes_accessed=int(8e6), transcendentals=0)
    light = pl.CostEstimate(flops=int(1e9), bytes_accessed=int(4e6), transcendentals=0)

    def slot_call(sel, erem, brem, lrem, total):
        return pl.pallas_call(
            lambda *refs: slot_kernel(*refs, scale=2.0 * sharpness * LOG2E / features),
            grid_spec=pltpu.PrefetchScalarGridSpec(
                num_scalar_prefetch=1,
                grid=(count_t,),
                in_specs=[
                    pl.BlockSpec((1, TILE, features), at_list),
                    pl.BlockSpec((TILE, features), whole),
                    pl.BlockSpec((1, TILE, 1), at_list),
                    pl.BlockSpec((1, TILE), whole),
                    pl.BlockSpec(block, at_list),
                    pl.BlockSpec((TILE, C), whole),
                    pl.BlockSpec(block, at_list),
                ],
                out_specs=[
                    pl.BlockSpec((1, TILE, TILE), at_place),
                    pl.BlockSpec((TILE, C), whole),
                    pl.BlockSpec(block, at_list),
                ],
            ),
            out_shape=[
                jax.ShapeDtypeStruct((count_t, TILE, TILE), jnp.bfloat16),
                jax.ShapeDtypeStruct((TILE, C), jnp.float32),
                jax.ShapeDtypeStruct((count_t, TILE, C), jnp.float32),
            ],
            input_output_aliases={7: 2},
            cost_estimate=estimate,
            name="slot",
        )(sel, tiles, erem, bias_column, brem, rounded, lrem, total)

    def push_call(sel, kernel, own):
        return pl.pallas_call(
            push_kernel,
            grid_spec=pltpu.PrefetchScalarGridSpec(
                num_scalar_prefetch=1,
                grid=(count_t,),
                in_specs=[pl.BlockSpec((1, TILE, TILE), at_place), pl.BlockSpec(block, at_list)],
                out_specs=pl.BlockSpec((TILE, C), whole),
            ),
            out_shape=jax.ShapeDtypeStruct((TILE, C), jnp.float32),
            cost_estimate=light,
            name="push",
        )(sel, kernel, own)

    def gather_call(sel, kernel, lrem, total):
        return pl.pallas_call(
            gather_kernel,
            grid_spec=pltpu.PrefetchScalarGridSpec(
                num_scalar_prefetch=1,
                grid=(count_t,),
                in_specs=[
                    pl.BlockSpec((1, TILE, TILE), at_place),
                    pl.BlockSpec((TILE, C), whole),
                    pl.BlockSpec(block, at_list),
                ],
                out_specs=pl.BlockSpec(block, at_list),
            ),
            out_shape=jax.ShapeDtypeStruct((count_t, TILE, C), jnp.float32),
            input_output_aliases={3: 0},
            cost_estimate=light,
            name="gather",
        )(sel, kernel, lrem, total)

    def add_push(total, arrived, slot):
        place = (mine[slot], 0, 0)
        old = lax.dynamic_slice(total, place, (1, TILE, C))
        return lax.dynamic_update_slice(total, old + arrived.astype(jnp.float32)[None], place)

    def slice_of(array, index):
        return lax.dynamic_index_in_dim(array, index, 0, keepdims=False)

    zeros = jnp.zeros((count_t, TILE, C), jnp.float32)
    degree = None

    gathered, returned = zeros, zeros
    received = []
    for k, s in enumerate(order):
        out = slice_of(tiles, mine[me ^ s])
        if k >= WINDOW:
            out, received[k - WINDOW] = lax.optimization_barrier((out, received[k - WINDOW]))
        received.append(swap(out, s))
    kernels, selections = {}, {}
    pushes = []
    for k, s in enumerate(order):
        peer = me ^ s
        sel = slice_of(selection, peer)
        remote_meta = slice_of(meta_in, peer)
        kernel, push, gathered = slot_call(
            sel, received[k], remote_meta[:1], slice_of(rounded_in, peer), gathered
        )
        kernels[s], selections[s] = kernel, sel
        pushes.append(swap(push.astype(jnp.float16), s))
    for k, s in enumerate(order):
        returned = add_push(returned, pushes[k], me ^ s)

    def update(labels, summed, degree):
        averaged = (labels + summed) / degree
        blended = mixing * averaged + (1.0 - mixing) * target
        squared = blended * blended
        return squared / jnp.sum(squared, axis=2, keepdims=True)

    summed = gathered + returned
    degree = 1.0 + jnp.sum(summed, axis=2, keepdims=True)
    labels = update(labels, summed, degree)

    for _ in range(1, ITERS):
        rounded = labels.astype(jnp.bfloat16)
        gathered, returned = zeros, zeros
        incoming, pushes = [], []
        for k, s in enumerate(order):
            out = slice_of(rounded, mine[me ^ s])
            push = push_call(selections[s], kernels[s], rounded).astype(jnp.float16)
            if k >= WINDOW:
                out, incoming[k - WINDOW] = lax.optimization_barrier((out, incoming[k - WINDOW]))
                push, pushes[k - WINDOW] = lax.optimization_barrier((push, pushes[k - WINDOW]))
            incoming.append(swap(out, s))
            pushes.append(swap(push, s))
        for k, s in enumerate(order):
            gathered = gather_call(selections[s], kernels[s], incoming[k], gathered)
            returned = add_push(returned, pushes[k], me ^ s)
        labels = update(labels, gathered + returned, degree)
    return labels.reshape(embed.shape[0], C)


def solution(mesh):
    in_specs = (
        P(("groups", "shard"), None),
        P(("groups", "shard")),
        P(("groups", "shard")),
        P(("groups", "shard"), None),
        P(("groups", "shard")),
        P(("groups", "shard")),
    )
    out_specs = P(("groups", "shard"), None)
    return jax.shard_map(body, mesh=mesh, in_specs=in_specs, out_specs=out_specs, check_vma=False)
```

```python
import math

import jax
import jax.numpy as jnp
from jax import lax
from jax.experimental import pallas as pl
from jax.experimental.pallas import tpu as pltpu
from jax.sharding import PartitionSpec as P

C = 256
TILE = 256
ITERS = 2
WINDOW = 4

sharpness = 1.0
mixing = 0.8

LOG2E = math.log2(math.e)
ANY = pl.BlockSpec(memory_space=pl.ANY)

PEER, MINE, COUNT, START, LIST = 0, 1, 2, 3, 4


def take_kernel(table, src, *rest, slots):
    outs, sem = rest[:-1], rest[-1]
    copies = [
        pltpu.make_async_copy(src.at[table[s, MINE]], out, sem.at[k])
        for k, (s, out) in enumerate(zip(slots, outs))
    ]
    for copy in copies:
        copy.start()
    for copy in copies:
        copy.wait()


def spread_kernel(mine, src, out, sem):
    copies = [
        pltpu.make_async_copy(src.at[mine[k]], out.at[k], sem.at[k]) for k in range(out.shape[0])
    ]
    for copy in copies:
        copy.start()
    for copy in copies:
        copy.wait()


def slot_kernel(table, eloc, erem, bloc, meta, lloc, *rest, slot, scale):
    kout, pout = rest[-2:]
    step = pl.program_id(0)

    @pl.when(step == 0)
    def _():
        pout[...] = jnp.zeros_like(pout)

    @pl.when(step < table[slot, COUNT])
    def _():
        inner = lax.dot_general(
            eloc[0], erem[...], (((1,), (1,)), ((), ())), preferred_element_type=jnp.float32
        )
        k = jnp.exp2(inner * scale + (bloc[0] + meta[0, :1])).astype(jnp.bfloat16)
        kout[0] = k
        pout[0] += lax.dot_general(
            k, lloc[0], (((0,), (0,)), ((), ())), preferred_element_type=jnp.float32
        )


def push_kernel(pairs, kref, lloc, unused, pout):
    step = pl.program_id(0)

    @pl.when((step == 0) | (pairs[0, step] != pairs[0, jnp.maximum(step - 1, 0)]))
    def _():
        pout[...] = jnp.zeros_like(pout)

    pout[0] += lax.dot_general(
        kref[0], lloc[pairs[1, step]], (((0,), (0,)), ((), ())), preferred_element_type=jnp.float32
    )


def gather_kernel(pairs, kref, lrem, gout):
    step = pl.program_id(0)

    @pl.when(step == 0)
    def _():
        gout[...] = jnp.zeros_like(gout)

    gout[pairs[1, step]] += jnp.dot(kref[0], lrem[0], preferred_element_type=jnp.float32)


def update_kernel(mine, gathered, back, old, target, *rest, first):
    if first:
        degree, out, rounded, total = rest
    else:
        degree, out, total = rest
    tile = pl.program_id(0)
    total[...] = gathered[0]
    for k in range(back.shape[0]):

        @pl.when(mine[k] == tile)
        def _():
            total[...] += back[k]

    summed = total[...]
    if first:
        degree[0] = 1.0 + jnp.sum(summed, axis=1, keepdims=True)
    averaged = (old[0] + summed) / degree[0]
    blended = mixing * averaged + (1.0 - mixing) * target[0]
    squared = blended * blended
    labels = squared / jnp.sum(squared, axis=1, keepdims=True)
    out[0] = labels
    if first:
        rounded[0] = labels.astype(jnp.bfloat16)


def body(embed, seed_mask, seed_class, partner, pair_local, pair_peer):
    n = lax.axis_size("shard")
    me = lax.axis_index("shard")
    features = embed.shape[1]
    tiles = embed.reshape(-1, TILE, features)
    tile_count = tiles.shape[0]
    pair_count = pair_local.shape[0]
    mine = partner.reshape(-1)
    half = n // 2
    order = []
    for k in range(half):
        order.append(half + k)
        if k + 1 < half:
            order.append(k + 1)

    tile_ids = jnp.arange(tile_count, dtype=jnp.int32)
    slot_ids = jnp.arange(n, dtype=jnp.int32)
    peers = slot_ids ^ me
    pair_slot = pair_peer ^ me
    mine_x = jnp.sum(jnp.where(peers[:, None] == slot_ids[None, :], mine[None, :], 0), axis=1)
    sends = jnp.stack([peers, mine_x], axis=1)
    active = jnp.any(
        (pair_slot[None, None, :] == slot_ids[:, None, None])
        & (pair_local[None, None, :] == tile_ids[None, :, None]),
        axis=2,
    )
    counts = jnp.sum(active.astype(jnp.int32), axis=1)
    starts = jnp.sum((pair_slot[None, :] < slot_ids[:, None]).astype(jnp.int32), axis=1)
    place = jnp.sum(
        (active[:, None, :] & (tile_ids[None, None, :] < tile_ids[None, :, None])).astype(jnp.int32), axis=2
    )
    wanted = jnp.minimum(tile_ids[None, :], jnp.maximum(counts - 1, 0)[:, None])
    listed = jnp.sum(
        jnp.where(active[:, None, :] & (place[:, None, :] == wanted[:, :, None]), tile_ids[None, None, :], 0),
        axis=2,
    )
    table = jnp.concatenate([sends, counts[:, None], starts[:, None], listed], axis=1).astype(jnp.int32)
    key = pair_slot * tile_count + pair_local
    rank = jnp.sum((key[None, :] < key[:, None]).astype(jnp.int32), axis=1)
    chosen = rank[None, :] == jnp.arange(pair_count, dtype=jnp.int32)[:, None]
    pairs = jnp.stack(
        [
            jnp.sum(jnp.where(chosen, pair_peer[None, :], 0), axis=1),
            jnp.sum(jnp.where(chosen, pair_local[None, :], 0), axis=1),
        ]
    ).astype(jnp.int32)

    def take(slots):
        return pl.pallas_call(
            lambda *refs: take_kernel(*refs, slots=slots),
            grid_spec=pltpu.PrefetchScalarGridSpec(
                num_scalar_prefetch=1,
                grid=(1,),
                in_specs=[ANY],
                out_specs=[ANY] * len(slots),
                scratch_shapes=[pltpu.SemaphoreType.DMA((len(slots),))],
            ),
            out_shape=[jax.ShapeDtypeStruct((TILE, features), embed.dtype)] * len(slots),
            name="take",
        )(sends, tiles)

    outgoing = dict(zip(order[:3], take(order[:3])))
    outgoing.update(zip(order[3:], take(order[3:])))
    received = []
    for k, s in enumerate(order):
        out = outgoing[s]
        if k >= WINDOW:
            out, received[k - WINDOW] = lax.optimization_barrier((out, received[k - WINDOW]))
        received.append(lax.ppermute(out, "shard", [(q, q ^ s) for q in range(n)]))

    norms = jnp.sum(jnp.square(tiles.astype(jnp.float32)), axis=2)
    bias = (1.0 - norms * (1.0 / features)) * (sharpness * LOG2E)
    seeded = seed_mask == 1
    classes = jnp.where(seeded, seed_class, -1).reshape(tile_count, TILE).astype(jnp.float32)
    meta = jnp.stack([bias, classes], axis=1)
    meta_in = lax.all_to_all(meta[mine], "shard", split_axis=0, concat_axis=0, tiled=True)
    class_ids = jnp.arange(C, dtype=jnp.float32)

    def first_labels(ids):
        return jnp.where(ids[..., None] < 0, 1.0 / C, (ids[..., None] == class_ids).astype(jnp.float32))

    labels = first_labels(classes)
    target = jnp.where(seeded.reshape(tile_count, TILE)[..., None], labels, 0.0)
    rounded = labels.astype(jnp.bfloat16)
    rounded_in = first_labels(meta_in[:, 1]).astype(jnp.bfloat16)
    bias_column = bias[:, :, None]

    block = (1, TILE, C)
    square = (1, TILE, TILE)
    sums = jax.ShapeDtypeStruct((n, TILE, C), jnp.float32)
    tile_sums = jax.ShapeDtypeStruct((tile_count, TILE, C), jnp.float32)

    def slot_call(slot, erem, kernels, pushes):
        def listed_tile(g, t):
            return (t[slot, LIST + g], 0, 0)

        def kernel_place(g, t):
            last = jnp.maximum(t[slot, COUNT] - 1, 0)
            here = t[slot, START] + jnp.minimum(g, last)
            return (jnp.where(t[slot, COUNT] > 0, here, pair_count), 0, 0)

        def peer(g, t):
            return (t[slot, PEER], 0, 0)

        begun = [] if kernels is None else [kernels, pushes]
        return pl.pallas_call(
            lambda *refs: slot_kernel(*refs, slot=slot, scale=2.0 * sharpness * LOG2E / features),
            grid_spec=pltpu.PrefetchScalarGridSpec(
                num_scalar_prefetch=1,
                grid=(tile_count,),
                in_specs=[
                    pl.BlockSpec((1, TILE, features), listed_tile),
                    pl.BlockSpec((TILE, features), lambda g, t: (0, 0)),
                    pl.BlockSpec((1, TILE, 1), listed_tile),
                    pl.BlockSpec((1, 2, TILE), peer),
                    pl.BlockSpec(block, listed_tile),
                ]
                + [ANY] * len(begun),
                out_specs=[pl.BlockSpec(square, kernel_place), pl.BlockSpec(block, peer)],
            ),
            out_shape=[jax.ShapeDtypeStruct((pair_count + 1, TILE, TILE), jnp.bfloat16), sums],
            input_output_aliases={6: 0, 7: 1} if begun else {},
            cost_estimate=pl.CostEstimate(flops=int(2e9), bytes_accessed=int(8e6), transcendentals=0),
            name="slot",
        )(table, tiles, erem, bias_column, meta_in, rounded, *begun)

    def push_call(kernels, own):
        return pl.pallas_call(
            push_kernel,
            grid_spec=pltpu.PrefetchScalarGridSpec(
                num_scalar_prefetch=1,
                grid=(pair_count,),
                in_specs=[
                    pl.BlockSpec(square, lambda g, p: (g, 0, 0)),
                    pl.BlockSpec(own.shape, lambda g, p: (0, 0, 0)),
                    ANY,
                ],
                out_specs=pl.BlockSpec(block, lambda g, p: (p[0, g], 0, 0)),
            ),
            out_shape=sums,
            input_output_aliases={3: 0},
            cost_estimate=pl.CostEstimate(flops=int(2e10), bytes_accessed=int(6e7), transcendentals=0),
            name="push",
        )(pairs, kernels, own, jnp.zeros(sums.shape, sums.dtype))

    def gather_call(kernels, incoming):
        return pl.pallas_call(
            gather_kernel,
            grid_spec=pltpu.PrefetchScalarGridSpec(
                num_scalar_prefetch=1,
                grid=(pair_count,),
                in_specs=[
                    pl.BlockSpec(square, lambda g, p: (g, 0, 0)),
                    pl.BlockSpec(block, lambda g, p: (p[0, g], 0, 0)),
                ],
                out_specs=pl.BlockSpec(tile_sums.shape, lambda g, p: (0, 0, 0)),
            ),
            out_shape=tile_sums,
            cost_estimate=pl.CostEstimate(flops=int(2e10), bytes_accessed=int(6e7), transcendentals=0),
            name="gather",
        )(pairs, kernels, incoming)

    def update_call(gathered, back, old, degree):
        first = degree is None
        by_tile = pl.BlockSpec(block, lambda g, m: (g, 0, 0))
        column = pl.BlockSpec((1, TILE, 1), lambda g, m: (g, 0, 0))
        column_shape = jax.ShapeDtypeStruct((tile_count, TILE, 1), jnp.float32)
        return pl.pallas_call(
            lambda *refs: update_kernel(*refs, first=first),
            grid_spec=pltpu.PrefetchScalarGridSpec(
                num_scalar_prefetch=1,
                grid=(tile_count,),
                in_specs=[by_tile, pl.BlockSpec(back.shape, lambda g, m: (0, 0, 0)), by_tile, by_tile]
                + ([] if first else [column]),
                out_specs=[column, by_tile, by_tile] if first else by_tile,
                scratch_shapes=[pltpu.VMEM((TILE, C), jnp.float32)],
            ),
            out_shape=[column_shape, tile_sums, jax.ShapeDtypeStruct(tile_sums.shape, jnp.bfloat16)]
            if first
            else tile_sums,
            name="update",
        )(owners, gathered, back, old, target, *([] if first else [degree]))

    def spread(array):
        return pl.pallas_call(
            spread_kernel,
            grid_spec=pltpu.PrefetchScalarGridSpec(
                num_scalar_prefetch=1,
                grid=(1,),
                in_specs=[ANY],
                out_specs=ANY,
                scratch_shapes=[pltpu.SemaphoreType.DMA((n,))],
            ),
            out_shape=jax.ShapeDtypeStruct((n,) + array.shape[1:], array.dtype),
            name="spread",
        )(mine, array)

    def exchange(array):
        return lax.all_to_all(array, "shard", split_axis=0, concat_axis=0, tiled=True)

    owners = jnp.where(slot_ids == me, -1, mine)
    kernels = pushes = None
    for k, s in enumerate(order):
        kernels, pushes = slot_call(s, received[k], kernels, pushes)
    back = exchange(pushes.astype(jnp.float16)).astype(jnp.float32)
    gathered = gather_call(kernels, rounded_in)
    degree, labels, rounded = update_call(gathered, back, labels, None)
    for _ in range(1, ITERS):
        incoming = exchange(spread(rounded))
        pushes = push_call(kernels, rounded)
        back = exchange(pushes.astype(jnp.float16)).astype(jnp.float32)
        gathered = gather_call(kernels, incoming)
        labels = update_call(gathered, back, labels, degree)
    return labels.reshape(embed.shape[0], C)


def solution(mesh):
    in_specs = (
        P(("groups", "shard"), None),
        P(("groups", "shard")),
        P(("groups", "shard")),
        P(("groups", "shard"), None),
        P(("groups", "shard")),
        P(("groups", "shard")),
    )
    out_specs = P(("groups", "shard"), None)
    return jax.shard_map(body, mesh=mesh, in_specs=in_specs, out_specs=out_specs, check_vma=False)
```

```python
import math

import jax
import jax.numpy as jnp
from jax import lax
from jax.experimental import pallas as pl
from jax.experimental.pallas import tpu as pltpu
from jax.sharding import PartitionSpec as P

C = 256
TILE = 256
ITERS = 2
WINDOW = 4
FLIGHT = 5
BATCH = 4
VMEM = 40 * 1024 * 1024

sharpness = 1.0
mixing = 0.8

LOG2E = math.log2(math.e)
ANY = pl.BlockSpec(memory_space=pl.ANY)

PEER, MINE, COUNT, LIST = 0, 1, 2, 3


def take_kernel(table, src, *rest, first):
    outs, sem = rest[:-1], rest[-1]
    for k, out in enumerate(outs):

        @pl.when(pl.program_id(0) == k)
        def _():
            copy = pltpu.make_async_copy(src.at[0], out, sem)
            copy.start()
            copy.wait()


def batch_kernel(table, tiles, bias, meta, own, gin, *rest, slots, begin, scale):
    size = len(slots)
    erem, lrem = rest[:size], rest[size : 2 * size]
    kout, gout, pouts = rest[-2 - size], rest[-1 - size], rest[-size:]
    gout[...] = gin[...]
    for k, slot in enumerate(slots):
        pouts[k][...] = jnp.zeros_like(pouts[k])
        row = meta[table[slot, PEER]][:1]

        def pair(g, carry, k=k, slot=slot, row=row):
            tile = table[slot, LIST + g]
            inner = lax.dot_general(
                tiles[tile], erem[k][...], (((1,), (1,)), ((), ())), preferred_element_type=jnp.float32
            )
            kernel = jnp.exp2(inner * scale + (bias[tile] + row)).astype(jnp.bfloat16)
            kout[k * tiles.shape[0] + g] = kernel
            gout[tile] += jnp.dot(kernel, lrem[k][0], preferred_element_type=jnp.float32)
            pouts[k][...] += lax.dot_general(
                kernel, own[tile], (((0,), (0,)), ((), ())), preferred_element_type=jnp.float32
            )
            return carry

        lax.fori_loop(0, table[slot, COUNT], pair, 0)


def push_kernel(table, kref, own, pout):
    slot = pl.program_id(0)
    pout[...] = jnp.zeros_like(pout)

    def pair(g, carry):
        pout[0] += lax.dot_general(
            kref[g],
            own[table[slot, LIST + g]],
            (((0,), (0,)), ((), ())),
            preferred_element_type=jnp.float32,
        )
        return carry

    lax.fori_loop(0, table[slot, COUNT], pair, 0)


def gather_kernel(table, kref, lrem, gout):
    slot = pl.program_id(0)

    @pl.when(slot == 0)
    def _():
        gout[...] = jnp.zeros_like(gout)

    def pair(g, carry):
        gout[table[slot, LIST + g]] += jnp.dot(kref[g], lrem[0], preferred_element_type=jnp.float32)
        return carry

    lax.fori_loop(0, table[slot, COUNT], pair, 0)


def update_kernel(owners, mine, gathered, classes, *rest, count, first):
    tile = pl.program_id(0)
    backs, rest = rest[:count], rest[count:]
    if first:
        degree, out, send, total, rounded, sem = rest
    else:
        old, degree, out, total = rest
    total[...] = gathered[0]
    for k in range(owners.shape[0]):

        @pl.when(owners[k] == tile)
        def _():
            total[...] += backs[k][...] if first else backs[0][k]

    summed = total[...]
    ids = classes[0]
    target = (ids == lax.broadcasted_iota(jnp.int32, (TILE, C), 1).astype(jnp.float32)).astype(jnp.float32)
    if first:
        degree[0] = 1.0 + jnp.sum(summed, axis=1, keepdims=True)
        labels = jnp.where(ids < 0, 1.0 / C, target)
    else:
        labels = old[0]
    blended = (labels + summed) * (mixing / degree[0]) + (1.0 - mixing) * target
    squared = blended * blended
    labels = squared * (1.0 / jnp.sum(squared, axis=1, keepdims=True))
    out[0] = labels
    if first:
        rounded[tile] = labels.astype(jnp.bfloat16)

        @pl.when(tile == pl.num_programs(0) - 1)
        def _():
            copies = [
                pltpu.make_async_copy(rounded.at[mine[k]], send.at[k], sem.at[k])
                for k in range(send.shape[0])
            ]
            for copy in copies:
                copy.start()
            for copy in copies:
                copy.wait()


def body(embed, seed_mask, seed_class, partner, pair_local, pair_peer):
    n = lax.axis_size("shard")
    me = lax.axis_index("shard")
    features = embed.shape[1]
    tiles = embed.reshape(-1, TILE, features)
    tile_count = tiles.shape[0]
    mine = partner.reshape(-1)
    half = n // 2
    order = []
    for k in range(half):
        order.append(half + k)
        if k + 1 < half:
            order.append(k + 1)
    slot_count = len(order)
    batches = [list(range(b, min(b + BATCH, slot_count))) for b in range(0, slot_count, BATCH)]

    tile_ids = jnp.arange(tile_count, dtype=jnp.int32)
    shard_ids = jnp.arange(n, dtype=jnp.int32)
    peers = jnp.array(order, jnp.int32) ^ me
    mine_x = jnp.sum(jnp.where(peers[:, None] == shard_ids[None, :], mine[None, :], 0), axis=1)
    sends = jnp.stack([peers, mine_x], axis=1).astype(jnp.int32)
    active = jnp.any(
        (pair_peer[None, None, :] == peers[:, None, None])
        & (pair_local[None, None, :] == tile_ids[None, :, None]),
        axis=2,
    )
    counts = jnp.sum(active.astype(jnp.int32), axis=1)
    place = jnp.sum(
        (active[:, None, :] & (tile_ids[None, None, :] < tile_ids[None, :, None])).astype(jnp.int32), axis=2
    )
    listed = jnp.sum(
        jnp.where(
            active[:, None, :] & (place[:, None, :] == tile_ids[None, :, None]), tile_ids[None, None, :], 0
        ),
        axis=2,
    )
    table = jnp.concatenate([sends, counts[:, None], listed], axis=1).astype(jnp.int32)

    def swap(value, k):
        return lax.ppermute(value, "shard", [(q, q ^ order[k]) for q in range(n)])

    def take(slots):
        first, size = slots[0], len(slots)
        return pl.pallas_call(
            lambda *refs: take_kernel(*refs, first=first),
            grid_spec=pltpu.PrefetchScalarGridSpec(
                num_scalar_prefetch=1,
                grid=(size,),
                in_specs=[pl.BlockSpec((1, TILE, features), lambda g, t: (t[first + g, MINE], 0, 0))],
                out_specs=[ANY] * size,
                scratch_shapes=[pltpu.SemaphoreType.DMA],
            ),
            out_shape=[jax.ShapeDtypeStruct((TILE, features), embed.dtype)] * size,
            name="take",
        )(sends, tiles)

    outgoing = list(take(list(range(WINDOW)))) + list(take(list(range(WINDOW, slot_count))))
    flying = []
    for k in range(slot_count):
        out = outgoing[k]
        if k >= WINDOW:
            out, flying[k - WINDOW] = lax.optimization_barrier((out, flying[k - WINDOW]))
        flying.append(swap(out, k))

    norms = jnp.sum(jnp.square(tiles.astype(jnp.float32)), axis=2)
    bias = (1.0 - norms * (1.0 / features)) * (sharpness * LOG2E)
    classes = jnp.where(seed_mask == 1, seed_class, -1).reshape(tile_count, TILE).astype(jnp.float32)
    meta = jnp.stack([bias, classes], axis=1)
    meta_in = lax.all_to_all(meta[mine], "shard", split_axis=0, concat_axis=0, tiled=True)
    class_ids = jnp.arange(C, dtype=jnp.float32)

    def first_labels(ids):
        hot = (ids[..., None] == class_ids).astype(jnp.float32)
        return jnp.where(ids[..., None] < 0, 1.0 / C, hot).astype(jnp.bfloat16)

    own = first_labels(classes)
    own_in = first_labels(meta_in[:, 1])
    bias_column = bias[:, :, None]
    class_column = classes[:, :, None]

    block = (1, TILE, C)
    store = (tile_count, TILE, TILE)
    sums = jax.ShapeDtypeStruct((TILE, C), jnp.float32)
    all_sums = jax.ShapeDtypeStruct((n, TILE, C), jnp.float32)
    tile_sums = jax.ShapeDtypeStruct((tile_count, TILE, C), jnp.float32)
    kernel_store = jax.ShapeDtypeStruct((len(batches) * BATCH * tile_count, TILE, TILE), jnp.bfloat16)

    def full(array):
        return pl.BlockSpec(array.shape, lambda g, t: (0,) * len(array.shape))

    def by_peer(slot):
        return pl.BlockSpec(block, lambda g, t: (t[slot, PEER], 0, 0))

    def batch_call(index, erem, kernels, gathered):
        slots = batches[index]
        size = len(slots)
        begun = [] if kernels is None else [kernels]
        args = [tiles, bias_column, meta_in, own, gathered] + erem + [own_in] * size
        in_specs = [full(a) for a in args[: 5 + size]] + [by_peer(s) for s in slots]
        return pl.pallas_call(
            lambda *refs: batch_kernel(
                *refs, slots=slots, begin=slots[0], scale=2.0 * sharpness * LOG2E / features
            ),
            grid_spec=pltpu.PrefetchScalarGridSpec(
                num_scalar_prefetch=1,
                grid=(1,),
                in_specs=in_specs + [ANY] * len(begun),
                out_specs=[
                    pl.BlockSpec((BATCH * tile_count, TILE, TILE), lambda g, t: (index, 0, 0)),
                    full(tile_sums),
                ]
                + [full(sums)] * size,
            ),
            out_shape=[kernel_store, tile_sums] + [sums] * size,
            input_output_aliases={6 + 2 * size: 0} if begun else {},
            compiler_params=pltpu.CompilerParams(vmem_limit_bytes=VMEM),
            cost_estimate=pl.CostEstimate(flops=int(1e10), bytes_accessed=int(3e7), transcendentals=0),
            name="batch",
        )(table, *args, *begun)

    def push_call(kernels, own):
        return pl.pallas_call(
            push_kernel,
            grid_spec=pltpu.PrefetchScalarGridSpec(
                num_scalar_prefetch=1,
                grid=(slot_count,),
                in_specs=[pl.BlockSpec(store, lambda g, t: (g, 0, 0)), full(own)],
                out_specs=pl.BlockSpec(block, lambda g, t: (t[g, PEER], 0, 0)),
            ),
            out_shape=all_sums,
            compiler_params=pltpu.CompilerParams(vmem_limit_bytes=VMEM),
            cost_estimate=pl.CostEstimate(flops=int(2e10), bytes_accessed=int(6e7), transcendentals=0),
            name="push",
        )(table, kernels, own)

    def gather_call(kernels, incoming):
        return pl.pallas_call(
            gather_kernel,
            grid_spec=pltpu.PrefetchScalarGridSpec(
                num_scalar_prefetch=1,
                grid=(slot_count,),
                in_specs=[
                    pl.BlockSpec(store, lambda g, t: (g, 0, 0)),
                    pl.BlockSpec(block, lambda g, t: (t[g, PEER], 0, 0)),
                ],
                out_specs=full(tile_sums),
            ),
            out_shape=tile_sums,
            compiler_params=pltpu.CompilerParams(vmem_limit_bytes=VMEM),
            cost_estimate=pl.CostEstimate(flops=int(2e10), bytes_accessed=int(6e7), transcendentals=0),
            name="gather",
        )(table, kernels, incoming)

    def update_call(owners, gathered, backs, state):
        first = state is None
        by_tile = pl.BlockSpec(block, lambda g, o, m: (g, 0, 0))
        column = pl.BlockSpec((1, TILE, 1), lambda g, o, m: (g, 0, 0))
        column_shape = jax.ShapeDtypeStruct((tile_count, TILE, 1), jnp.float32)
        back_specs = [pl.BlockSpec(b.shape, lambda g, o, m, d=len(b.shape): (0,) * d) for b in backs]
        out_shape, out_specs = [tile_sums], [by_tile]
        scratch = [pltpu.VMEM((TILE, C), jnp.float32)]
        if first:
            send = jax.ShapeDtypeStruct((n, TILE, C), jnp.bfloat16)
            out_shape, out_specs = [column_shape, tile_sums, send], [column, by_tile, ANY]
            scratch += [
                pltpu.VMEM((tile_count, TILE, C), jnp.bfloat16),
                pltpu.SemaphoreType.DMA((n,)),
            ]
        return pl.pallas_call(
            lambda *refs: update_kernel(*refs, count=len(backs), first=first),
            grid_spec=pltpu.PrefetchScalarGridSpec(
                num_scalar_prefetch=2,
                grid=(tile_count,),
                in_specs=[by_tile, column] + back_specs + ([] if first else [by_tile, column]),
                out_specs=out_specs,
                scratch_shapes=scratch,
            ),
            out_shape=out_shape,
            compiler_params=pltpu.CompilerParams(vmem_limit_bytes=VMEM),
            name="update",
        )(owners, mine, gathered, class_column, *backs, *([] if first else state))

    def exchange(array):
        return lax.all_to_all(array, "shard", split_axis=0, concat_axis=0, tiled=True)

    kernels, gathered = None, jnp.zeros(tile_sums.shape, tile_sums.dtype)
    pushes = []
    for b, slots in enumerate(batches):
        kernels, gathered, *done = batch_call(b, [flying[k] for k in slots], kernels, gathered)
        pushes += done
    for k in range(slot_count):
        out = pushes[k].astype(jnp.float16)
        ahead = slot_count + k - FLIGHT
        out, flying[ahead] = lax.optimization_barrier((out, flying[ahead]))
        flying.append(swap(out, k))
    backs = [back.astype(jnp.float32) for back in flying[slot_count:]]
    degree, labels, send = update_call(mine_x, gathered, backs, None)

    incoming = exchange(send)
    rounded = labels.astype(jnp.bfloat16)
    pushes = push_call(kernels, rounded)
    back = exchange(pushes.astype(jnp.float16)).astype(jnp.float32)
    gathered = gather_call(kernels, incoming)
    owners = jnp.where(shard_ids == me, -1, mine)
    (labels,) = update_call(owners, gathered, [back], [labels, degree])
    return labels.reshape(embed.shape[0], C)


def solution(mesh):
    in_specs = (
        P(("groups", "shard"), None),
        P(("groups", "shard")),
        P(("groups", "shard")),
        P(("groups", "shard"), None),
        P(("groups", "shard")),
        P(("groups", "shard")),
    )
    out_specs = P(("groups", "shard"), None)
    return jax.shard_map(body, mesh=mesh, in_specs=in_specs, out_specs=out_specs, check_vma=False)
```

```python
import math

import jax
import jax.numpy as jnp
from jax import lax
from jax.experimental import pallas as pl
from jax.experimental.pallas import tpu as pltpu
from jax.sharding import PartitionSpec as P

C = 256
TILE = 256
ITERS = 2
WINDOW = 8
FLIGHT = 8
BATCH = 4
VMEM = 40 * 1024 * 1024

sharpness = 1.0
mixing = 0.8

LOG2E = math.log2(math.e)
ANY = pl.BlockSpec(memory_space=pl.ANY)

PEER, MINE, COUNT, LIST = 0, 1, 2, 3


def take_kernel(mine, me, src, *rest, peers):
    size = len(peers)
    outs, stage, arrive, leave = rest[:size], rest[size], rest[size + 1], rest[size + 2]
    loads = [
        pltpu.make_async_copy(src.at[mine[me[0] ^ peer]], stage.at[k], arrive.at[k])
        for k, peer in enumerate(peers)
    ]
    stores = [pltpu.make_async_copy(stage.at[k], out, leave.at[k]) for k, out in enumerate(outs)]
    for load in loads:
        load.start()
    for load, store in zip(loads, stores):
        load.wait()
        store.start()
    for store in stores:
        store.wait()


def batch_kernel(table, tiles, bias, meta, own, gin, *rest, slots, begin, scale):
    size = len(slots)
    erem, lrem = rest[:size], rest[size : 2 * size]
    kout, gout, pouts = rest[-2 - size], rest[-1 - size], rest[-size:]
    gout[...] = gin[...]
    for k, slot in enumerate(slots):
        pouts[k][...] = jnp.zeros_like(pouts[k])
        row = meta[table[slot, PEER]][:1]

        def pair(g, carry, k=k, slot=slot, row=row):
            tile = table[slot, LIST + g]
            inner = lax.dot_general(
                tiles[tile], erem[k][...], (((1,), (1,)), ((), ())), preferred_element_type=jnp.float32
            )
            kernel = jnp.exp2(inner * scale + (bias[tile] + row)).astype(jnp.bfloat16)
            kout[k * tiles.shape[0] + g] = kernel
            gout[tile] += jnp.dot(kernel, lrem[k][0], preferred_element_type=jnp.float32)
            pouts[k][...] += lax.dot_general(
                kernel, own[tile], (((0,), (0,)), ((), ())), preferred_element_type=jnp.float32
            )
            return carry

        lax.fori_loop(0, table[slot, COUNT], pair, 0)


def push_kernel(table, kref, own, pout):
    slot = pl.program_id(0)
    pout[...] = jnp.zeros_like(pout)

    def pair(g, carry):
        pout[0] += lax.dot_general(
            kref[g],
            own[table[slot, LIST + g]],
            (((0,), (0,)), ((), ())),
            preferred_element_type=jnp.float32,
        )
        return carry

    lax.fori_loop(0, table[slot, COUNT], pair, 0)


def gather_kernel(table, kref, lrem, gout):
    slot = pl.program_id(0)

    @pl.when(slot == 0)
    def _():
        gout[...] = jnp.zeros_like(gout)

    def pair(g, carry):
        gout[table[slot, LIST + g]] += jnp.dot(kref[g], lrem[0], preferred_element_type=jnp.float32)
        return carry

    lax.fori_loop(0, table[slot, COUNT], pair, 0)


def update_kernel(owners, mine, gathered, classes, *rest, count, first):
    tile = pl.program_id(0)
    backs, rest = rest[:count], rest[count:]
    if first:
        degree, out, send, total, rounded, sem = rest
    else:
        old, degree, out, total = rest
    total[...] = gathered[0]
    for k in range(owners.shape[0]):

        @pl.when(owners[k] == tile)
        def _():
            total[...] += backs[k][...] if first else backs[0][k]

    summed = total[...]
    ids = classes[0]
    target = (ids == lax.broadcasted_iota(jnp.int32, (TILE, C), 1).astype(jnp.float32)).astype(jnp.float32)
    if first:
        degree[0] = 1.0 + jnp.sum(summed, axis=1, keepdims=True)
        labels = jnp.where(ids < 0, 1.0 / C, target)
    else:
        labels = old[0]
    blended = (labels + summed) * (mixing / degree[0]) + (1.0 - mixing) * target
    squared = blended * blended
    labels = squared * (1.0 / jnp.sum(squared, axis=1, keepdims=True))
    out[0] = labels
    if first:
        rounded[tile] = labels.astype(jnp.bfloat16)

        @pl.when(tile == pl.num_programs(0) - 1)
        def _():
            copies = [
                pltpu.make_async_copy(rounded.at[mine[k]], send.at[k], sem.at[k])
                for k in range(send.shape[0])
            ]
            for copy in copies:
                copy.start()
            for copy in copies:
                copy.wait()


def body(embed, seed_mask, seed_class, partner, pair_local, pair_peer):
    n = lax.axis_size("shard")
    me = lax.axis_index("shard")
    features = embed.shape[1]
    tiles = embed.reshape(-1, TILE, features)
    tile_count = tiles.shape[0]
    mine = partner.reshape(-1)
    half = n // 2
    order = []
    for k in range(half):
        order.append(half + k)
        if k + 1 < half:
            order.append(k + 1)
    slot_count = len(order)
    batches = [list(range(b, min(b + BATCH, slot_count))) for b in range(0, slot_count, BATCH)]

    tile_ids = jnp.arange(tile_count, dtype=jnp.int32)
    shard_ids = jnp.arange(n, dtype=jnp.int32)
    peers = jnp.array(order, jnp.int32) ^ me
    mine_x = jnp.sum(jnp.where(peers[:, None] == shard_ids[None, :], mine[None, :], 0), axis=1)
    sends = jnp.stack([peers, mine_x], axis=1).astype(jnp.int32)
    active = jnp.any(
        (pair_peer[None, None, :] == peers[:, None, None])
        & (pair_local[None, None, :] == tile_ids[None, :, None]),
        axis=2,
    )
    counts = jnp.sum(active.astype(jnp.int32), axis=1)
    place = jnp.sum(
        (active[:, None, :] & (tile_ids[None, None, :] < tile_ids[None, :, None])).astype(jnp.int32), axis=2
    )
    listed = jnp.sum(
        jnp.where(
            active[:, None, :] & (place[:, None, :] == tile_ids[None, :, None]), tile_ids[None, None, :], 0
        ),
        axis=2,
    )
    table = jnp.concatenate([sends, counts[:, None], listed], axis=1).astype(jnp.int32)

    def swap(value, k):
        return lax.ppermute(value, "shard", [(q, q ^ order[k]) for q in range(n)])

    def take(slots):
        size = len(slots)
        return pl.pallas_call(
            lambda *refs: take_kernel(*refs, peers=[order[k] for k in slots]),
            grid_spec=pltpu.PrefetchScalarGridSpec(
                num_scalar_prefetch=2,
                grid=(1,),
                in_specs=[ANY],
                out_specs=[ANY] * size,
                scratch_shapes=[
                    pltpu.VMEM((size, TILE, features), embed.dtype),
                    pltpu.SemaphoreType.DMA((size,)),
                    pltpu.SemaphoreType.DMA((size,)),
                ],
            ),
            out_shape=[jax.ShapeDtypeStruct((TILE, features), embed.dtype)] * size,
            name="take",
        )(mine, me.reshape(1), tiles)

    outgoing = list(take(list(range(WINDOW)))) + list(take(list(range(WINDOW, slot_count))))
    flying = []
    for k in range(slot_count):
        out = outgoing[k]
        if k >= WINDOW:
            out, flying[k - WINDOW] = lax.optimization_barrier((out, flying[k - WINDOW]))
        flying.append(swap(out, k))

    norms = jnp.sum(jnp.square(tiles.astype(jnp.float32)), axis=2)
    bias = (1.0 - norms * (1.0 / features)) * (sharpness * LOG2E)
    classes = jnp.where(seed_mask == 1, seed_class, -1).reshape(tile_count, TILE).astype(jnp.float32)
    meta = jnp.stack([bias, classes], axis=1)
    meta_in = lax.all_to_all(meta[mine], "shard", split_axis=0, concat_axis=0, tiled=True)
    class_ids = jnp.arange(C, dtype=jnp.float32)

    def first_labels(ids):
        hot = (ids[..., None] == class_ids).astype(jnp.float32)
        return jnp.where(ids[..., None] < 0, 1.0 / C, hot).astype(jnp.bfloat16)

    own = first_labels(classes)
    own_in = first_labels(meta_in[:, 1])
    bias_column = bias[:, :, None]
    class_column = classes[:, :, None]

    block = (1, TILE, C)
    store = (tile_count, TILE, TILE)
    sums = jax.ShapeDtypeStruct((TILE, C), jnp.float32)
    all_sums = jax.ShapeDtypeStruct((n, TILE, C), jnp.float32)
    tile_sums = jax.ShapeDtypeStruct((tile_count, TILE, C), jnp.float32)
    kernel_store = jax.ShapeDtypeStruct((len(batches) * BATCH * tile_count, TILE, TILE), jnp.bfloat16)

    def full(array):
        return pl.BlockSpec(array.shape, lambda g, t: (0,) * len(array.shape))

    def by_peer(slot):
        return pl.BlockSpec(block, lambda g, t: (t[slot, PEER], 0, 0))

    def batch_call(index, erem, kernels, gathered):
        slots = batches[index]
        size = len(slots)
        begun = [] if kernels is None else [kernels]
        args = [tiles, bias_column, meta_in, own, gathered] + erem + [own_in] * size
        in_specs = [full(a) for a in args[: 5 + size]] + [by_peer(s) for s in slots]
        return pl.pallas_call(
            lambda *refs: batch_kernel(
                *refs, slots=slots, begin=slots[0], scale=2.0 * sharpness * LOG2E / features
            ),
            grid_spec=pltpu.PrefetchScalarGridSpec(
                num_scalar_prefetch=1,
                grid=(1,),
                in_specs=in_specs + [ANY] * len(begun),
                out_specs=[
                    pl.BlockSpec((BATCH * tile_count, TILE, TILE), lambda g, t: (index, 0, 0)),
                    full(tile_sums),
                ]
                + [full(sums)] * size,
            ),
            out_shape=[kernel_store, tile_sums] + [sums] * size,
            input_output_aliases={6 + 2 * size: 0} if begun else {},
            compiler_params=pltpu.CompilerParams(vmem_limit_bytes=VMEM),
            cost_estimate=pl.CostEstimate(flops=int(1e10), bytes_accessed=int(3e7), transcendentals=0),
            name="batch",
        )(table, *args, *begun)

    def push_call(kernels, own):
        return pl.pallas_call(
            push_kernel,
            grid_spec=pltpu.PrefetchScalarGridSpec(
                num_scalar_prefetch=1,
                grid=(slot_count,),
                in_specs=[pl.BlockSpec(store, lambda g, t: (g, 0, 0)), full(own)],
                out_specs=pl.BlockSpec(block, lambda g, t: (t[g, PEER], 0, 0)),
            ),
            out_shape=all_sums,
            compiler_params=pltpu.CompilerParams(vmem_limit_bytes=VMEM),
            cost_estimate=pl.CostEstimate(flops=int(2e10), bytes_accessed=int(6e7), transcendentals=0),
            name="push",
        )(table, kernels, own)

    def gather_call(kernels, incoming):
        return pl.pallas_call(
            gather_kernel,
            grid_spec=pltpu.PrefetchScalarGridSpec(
                num_scalar_prefetch=1,
                grid=(slot_count,),
                in_specs=[
                    pl.BlockSpec(store, lambda g, t: (g, 0, 0)),
                    pl.BlockSpec(block, lambda g, t: (t[g, PEER], 0, 0)),
                ],
                out_specs=full(tile_sums),
            ),
            out_shape=tile_sums,
            compiler_params=pltpu.CompilerParams(vmem_limit_bytes=VMEM),
            cost_estimate=pl.CostEstimate(flops=int(2e10), bytes_accessed=int(6e7), transcendentals=0),
            name="gather",
        )(table, kernels, incoming)

    def update_call(owners, gathered, backs, state):
        first = state is None
        by_tile = pl.BlockSpec(block, lambda g, o, m: (g, 0, 0))
        column = pl.BlockSpec((1, TILE, 1), lambda g, o, m: (g, 0, 0))
        column_shape = jax.ShapeDtypeStruct((tile_count, TILE, 1), jnp.float32)
        back_specs = [pl.BlockSpec(b.shape, lambda g, o, m, d=len(b.shape): (0,) * d) for b in backs]
        out_shape, out_specs = [tile_sums], [by_tile]
        scratch = [pltpu.VMEM((TILE, C), jnp.float32)]
        if first:
            send = jax.ShapeDtypeStruct((n, TILE, C), jnp.bfloat16)
            out_shape, out_specs = [column_shape, tile_sums, send], [column, by_tile, ANY]
            scratch += [
                pltpu.VMEM((tile_count, TILE, C), jnp.bfloat16),
                pltpu.SemaphoreType.DMA((n,)),
            ]
        return pl.pallas_call(
            lambda *refs: update_kernel(*refs, count=len(backs), first=first),
            grid_spec=pltpu.PrefetchScalarGridSpec(
                num_scalar_prefetch=2,
                grid=(tile_count,),
                in_specs=[by_tile, column] + back_specs + ([] if first else [by_tile, column]),
                out_specs=out_specs,
                scratch_shapes=scratch,
            ),
            out_shape=out_shape,
            compiler_params=pltpu.CompilerParams(vmem_limit_bytes=VMEM),
            name="update",
        )(owners, mine, gathered, class_column, *backs, *([] if first else state))

    def exchange(array):
        return lax.all_to_all(array, "shard", split_axis=0, concat_axis=0, tiled=True)

    kernels, gathered = None, jnp.zeros(tile_sums.shape, tile_sums.dtype)
    pushes = []
    for b, slots in enumerate(batches):
        kernels, gathered, *done = batch_call(b, [flying[k] for k in slots], kernels, gathered)
        pushes += done
    for k in range(slot_count):
        out = pushes[k].astype(jnp.float16)
        ahead = slot_count + k - FLIGHT
        out, flying[ahead] = lax.optimization_barrier((out, flying[ahead]))
        flying.append(swap(out, k))
    backs = [back.astype(jnp.float32) for back in flying[slot_count:]]
    degree, labels, send = update_call(mine_x, gathered, backs, None)

    incoming = exchange(send)
    rounded = labels.astype(jnp.bfloat16)
    pushes = push_call(kernels, rounded)
    pushes, incoming = lax.optimization_barrier((pushes.astype(jnp.float16), incoming))
    back = exchange(pushes).astype(jnp.float32)
    gathered = gather_call(kernels, incoming)
    owners = jnp.where(shard_ids == me, -1, mine)
    (labels,) = update_call(owners, gathered, [back], [labels, degree])
    return labels.reshape(embed.shape[0], C)


def solution(mesh):
    in_specs = (
        P(("groups", "shard"), None),
        P(("groups", "shard")),
        P(("groups", "shard")),
        P(("groups", "shard"), None),
        P(("groups", "shard")),
        P(("groups", "shard")),
    )
    out_specs = P(("groups", "shard"), None)
    return jax.shard_map(body, mesh=mesh, in_specs=in_specs, out_specs=out_specs, check_vma=False)
```

```python
import math

import jax
import jax.numpy as jnp
from jax import lax
from jax.experimental import pallas as pl
from jax.experimental.pallas import tpu as pltpu
from jax.sharding import PartitionSpec as P

C = 256
TILE = 256
ITERS = 2
WINDOW = 8
AFTER = 3
FLIGHT = 8
HOLD = 12
BATCH = 4
VMEM = 40 * 1024 * 1024

sharpness = 1.0
mixing = 0.8

LOG2E = math.log2(math.e)
ANY = pl.BlockSpec(memory_space=pl.ANY)

PEER, MINE, COUNT, LIST = 0, 1, 2, 3


def take_kernel(mine, me, src, *rest, peers):
    size = len(peers)
    outs, stage, arrive, leave = rest[:size], rest[size], rest[size + 1], rest[size + 2]
    loads = [
        pltpu.make_async_copy(src.at[mine[me[0] ^ peer]], stage.at[k], arrive.at[k])
        for k, peer in enumerate(peers)
    ]
    stores = [pltpu.make_async_copy(stage.at[k], out, leave.at[k]) for k, out in enumerate(outs)]
    for load in loads:
        load.start()
    for load, store in zip(loads, stores):
        load.wait()
        store.start()
    for store in stores:
        store.wait()


def batch_kernel(table, tiles, bias, meta, own, *rest, slots, begun, scale):
    size = len(slots)
    erem, lrem = rest[:size], rest[size : 2 * size]
    kout, gout, pouts = rest[-2 - size], rest[-1 - size], rest[-size:]
    gout[...] = rest[2 * size][...] if begun else own[...].astype(jnp.float32)
    for k, slot in enumerate(slots):
        pouts[k][...] = jnp.zeros_like(pouts[k])
        row = meta[table[slot, PEER]][:1]

        def pair(g, carry, k=k, slot=slot, row=row):
            tile = table[slot, LIST + g]
            inner = lax.dot_general(
                tiles[tile], erem[k][...], (((1,), (1,)), ((), ())), preferred_element_type=jnp.float32
            )
            kernel = jnp.exp2(inner * scale + (bias[tile] + row)).astype(jnp.bfloat16)
            kout[k * tiles.shape[0] + g] = kernel
            gout[tile] += jnp.dot(kernel, lrem[k][0], preferred_element_type=jnp.float32)
            pouts[k][...] += lax.dot_general(
                kernel, own[tile], (((0,), (0,)), ((), ())), preferred_element_type=jnp.float32
            )
            return carry

        lax.fori_loop(0, table[slot, COUNT], pair, 0)


def push_kernel(table, kref, own, pout):
    slot = pl.program_id(0)
    pout[...] = jnp.zeros_like(pout)

    def pair(g, carry):
        pout[0] += lax.dot_general(
            kref[g],
            own[table[slot, LIST + g]],
            (((0,), (0,)), ((), ())),
            preferred_element_type=jnp.float32,
        )
        return carry

    lax.fori_loop(0, table[slot, COUNT], pair, 0)


def gather_kernel(table, kref, lrem, labels, gout):
    slot = pl.program_id(0)

    @pl.when(slot == 0)
    def _():
        gout[...] = labels[...]

    def pair(g, carry):
        gout[table[slot, LIST + g]] += jnp.dot(kref[g], lrem[0], preferred_element_type=jnp.float32)
        return carry

    lax.fori_loop(0, table[slot, COUNT], pair, 0)


def update_kernel(owners, mine, gathered, classes, *rest, count, first):
    backs, rest = rest[:count], rest[count:]
    if first:
        shares, out, send, total, arrived, arrive, rounded, leave = rest
    else:
        shares, out, total, arrived, arrive = rest
    tile = pl.program_id(0)

    def load(k):
        source = backs[k] if first else backs[0].at[k]
        return pltpu.make_async_copy(source, arrived.at[k], arrive.at[k])

    def store(k):
        return pltpu.make_async_copy(rounded.at[mine[k]], send.at[k], leave.at[k])

    slots = range(owners.shape[0])

    @pl.when(tile == 0)
    def _():
        for k in slots:

            @pl.when(owners[k] >= 0)
            def _(k=k):
                load(k).start()

    total[...] = gathered[0]
    for k in slots:

        @pl.when(owners[k] == tile)
        def _(k=k):
            load(k).wait()
            total[...] += arrived[k]

    summed = total[...]
    diagonal = lax.broadcasted_iota(jnp.int32, (TILE, TILE), 0) == lax.broadcasted_iota(
        jnp.int32, (TILE, TILE), 1
    )
    ids = jnp.sum(jnp.where(diagonal, classes[0], 0.0), axis=1, keepdims=True)
    hot = ids == lax.broadcasted_iota(jnp.int32, (TILE, C), 1).astype(jnp.float32)
    if first:
        share = mixing / jnp.sum(summed, axis=1, keepdims=True)
        shares[0] = jnp.sum(jnp.where(diagonal, share, 0.0), axis=0, keepdims=True)
    else:
        share = jnp.sum(jnp.where(diagonal, shares[0], 0.0), axis=1, keepdims=True)
    blended = summed * share + jnp.where(hot, 1.0 - mixing, 0.0)
    squared = blended * blended
    labels = squared * (1.0 / jnp.sum(squared, axis=1, keepdims=True))
    out[0] = labels
    if first:
        rounded[tile] = labels.astype(jnp.bfloat16)
        for k in range(send.shape[0]):

            @pl.when(mine[k] == tile)
            def _(k=k):
                store(k).start()

        @pl.when(tile == pl.num_programs(0) - 1)
        def _():
            for k in range(send.shape[0]):
                store(k).wait()


def body(embed, seed_mask, seed_class, partner, pair_local, pair_peer):
    n = lax.axis_size("shard")
    me = lax.axis_index("shard")
    features = embed.shape[1]
    tiles = embed.reshape(-1, TILE, features)
    tile_count = tiles.shape[0]
    mine = partner.reshape(-1)
    half = n // 2
    order = []
    for k in range(half):
        order.append(half + k)
        if k + 1 < half:
            order.append(k + 1)
    slot_count = len(order)
    batches = [list(range(b, min(b + BATCH, slot_count))) for b in range(0, slot_count, BATCH)]

    tile_ids = jnp.arange(tile_count, dtype=jnp.int32)
    shard_ids = jnp.arange(n, dtype=jnp.int32)
    peers = jnp.array(order, jnp.int32) ^ me
    mine_x = jnp.sum(jnp.where(peers[:, None] == shard_ids[None, :], mine[None, :], 0), axis=1)
    sends = jnp.stack([peers, mine_x], axis=1).astype(jnp.int32)
    active = jnp.any(
        (pair_peer[None, None, :] == peers[:, None, None])
        & (pair_local[None, None, :] == tile_ids[None, :, None]),
        axis=2,
    )
    counts = jnp.sum(active.astype(jnp.int32), axis=1)
    place = jnp.sum(
        (active[:, None, :] & (tile_ids[None, None, :] < tile_ids[None, :, None])).astype(jnp.int32), axis=2
    )
    listed = jnp.sum(
        jnp.where(
            active[:, None, :] & (place[:, None, :] == tile_ids[None, :, None]), tile_ids[None, None, :], 0
        ),
        axis=2,
    )
    table = jnp.concatenate([sends, counts[:, None], listed], axis=1).astype(jnp.int32)

    def swap(value, k):
        return lax.ppermute(value, "shard", [(q, q ^ order[k]) for q in range(n)])

    def take(slots):
        size = len(slots)
        return pl.pallas_call(
            lambda *refs: take_kernel(*refs, peers=[order[k] for k in slots]),
            grid_spec=pltpu.PrefetchScalarGridSpec(
                num_scalar_prefetch=2,
                grid=(1,),
                in_specs=[ANY],
                out_specs=[ANY] * size,
                scratch_shapes=[
                    pltpu.VMEM((size, TILE, features), embed.dtype),
                    pltpu.SemaphoreType.DMA((size,)),
                    pltpu.SemaphoreType.DMA((size,)),
                ],
            ),
            out_shape=[jax.ShapeDtypeStruct((TILE, features), embed.dtype)] * size,
            name="take",
        )(mine, me.reshape(1), tiles)

    outgoing = list(take(list(range(WINDOW)))) + list(take(list(range(WINDOW, slot_count))))
    flying = []
    for k in range(slot_count):
        out = outgoing[k]
        if k >= WINDOW:
            out, flying[k - WINDOW] = lax.optimization_barrier((out, flying[k - WINDOW]))
        flying.append(swap(out, k))

    norms = jnp.sum(jnp.square(tiles.astype(jnp.float32)), axis=2)
    bias = (1.0 - norms * (1.0 / features)) * (sharpness * LOG2E)
    classes = jnp.where(seed_mask == 1, seed_class, -1).reshape(tile_count, TILE).astype(jnp.float32)
    meta = jnp.stack([bias, classes], axis=1)
    meta_out, flying[AFTER] = lax.optimization_barrier((meta[mine], flying[AFTER]))
    meta_in = lax.all_to_all(meta_out, "shard", split_axis=0, concat_axis=0, tiled=True)
    class_ids = jnp.arange(C, dtype=jnp.float32)

    def first_labels(ids):
        hot = (ids[..., None] == class_ids).astype(jnp.float32)
        return jnp.where(ids[..., None] < 0, 1.0 / C, hot).astype(jnp.bfloat16)

    own = first_labels(classes)
    own_in = first_labels(meta_in[:, 1])
    bias_column = bias[:, :, None]
    class_rows = classes[:, None, :]

    block = (1, TILE, C)
    store = (tile_count, TILE, TILE)
    sums = jax.ShapeDtypeStruct((TILE, C), jnp.float32)
    all_sums = jax.ShapeDtypeStruct((n, TILE, C), jnp.float32)
    tile_sums = jax.ShapeDtypeStruct((tile_count, TILE, C), jnp.float32)
    kernel_store = jax.ShapeDtypeStruct((len(batches) * BATCH * tile_count, TILE, TILE), jnp.bfloat16)

    def full(array):
        return pl.BlockSpec(array.shape, lambda g, t: (0,) * len(array.shape))

    def by_peer(slot):
        return pl.BlockSpec(block, lambda g, t: (t[slot, PEER], 0, 0))

    def batch_call(index, erem, kernels, gathered):
        slots = batches[index]
        size = len(slots)
        args = [tiles, bias_column, meta_in, own] + erem + [own_in] * size
        in_specs = [full(a) for a in args[: 4 + size]] + [by_peer(s) for s in slots]
        aliases = {}
        if index:
            args += [gathered, kernels]
            in_specs += [full(tile_sums), ANY]
            aliases = {len(args): 0}
        return pl.pallas_call(
            lambda *refs: batch_kernel(
                *refs, slots=slots, begun=index > 0, scale=2.0 * sharpness * LOG2E / features
            ),
            grid_spec=pltpu.PrefetchScalarGridSpec(
                num_scalar_prefetch=1,
                grid=(1,),
                in_specs=in_specs,
                out_specs=[
                    pl.BlockSpec((BATCH * tile_count, TILE, TILE), lambda g, t: (index, 0, 0)),
                    full(tile_sums),
                ]
                + [full(sums)] * size,
            ),
            out_shape=[kernel_store, tile_sums] + [sums] * size,
            input_output_aliases=aliases,
            compiler_params=pltpu.CompilerParams(vmem_limit_bytes=VMEM),
            cost_estimate=pl.CostEstimate(flops=int(1e10), bytes_accessed=int(3e7), transcendentals=0),
            name="batch",
        )(table, *args)

    def push_call(kernels, own):
        return pl.pallas_call(
            push_kernel,
            grid_spec=pltpu.PrefetchScalarGridSpec(
                num_scalar_prefetch=1,
                grid=(slot_count,),
                in_specs=[pl.BlockSpec(store, lambda g, t: (g, 0, 0)), full(own)],
                out_specs=pl.BlockSpec(block, lambda g, t: (t[g, PEER], 0, 0)),
            ),
            out_shape=all_sums,
            compiler_params=pltpu.CompilerParams(vmem_limit_bytes=VMEM),
            cost_estimate=pl.CostEstimate(flops=int(2e10), bytes_accessed=int(6e7), transcendentals=0),
            name="push",
        )(table, kernels, own)

    def gather_call(kernels, incoming, labels):
        return pl.pallas_call(
            gather_kernel,
            grid_spec=pltpu.PrefetchScalarGridSpec(
                num_scalar_prefetch=1,
                grid=(slot_count,),
                in_specs=[
                    pl.BlockSpec(store, lambda g, t: (g, 0, 0)),
                    pl.BlockSpec(block, lambda g, t: (t[g, PEER], 0, 0)),
                    full(labels),
                ],
                out_specs=full(tile_sums),
            ),
            out_shape=tile_sums,
            compiler_params=pltpu.CompilerParams(vmem_limit_bytes=VMEM),
            cost_estimate=pl.CostEstimate(flops=int(2e10), bytes_accessed=int(6e7), transcendentals=0),
            name="gather",
        )(table, kernels, incoming, labels)

    def update_call(owners, gathered, backs, state):
        first = state is None
        by_tile = pl.BlockSpec(block, lambda g, o, m: (g, 0, 0))
        row = pl.BlockSpec((1, 1, TILE), lambda g, o, m: (g, 0, 0))
        out_shape, out_specs = [tile_sums], [by_tile]
        slots = owners.shape[0]
        scratch = [
            pltpu.VMEM((TILE, C), jnp.float32),
            pltpu.VMEM((slots, TILE, C), jnp.float32),
            pltpu.SemaphoreType.DMA((slots,)),
        ]
        if first:
            row_shape = jax.ShapeDtypeStruct((tile_count, 1, TILE), jnp.float32)
            out_shape = [row_shape, tile_sums, pltpu.HBM((n, TILE, C), jnp.bfloat16)]
            out_specs = [row, by_tile, pl.BlockSpec(memory_space=pltpu.HBM)]
            scratch += [
                pltpu.VMEM((tile_count, TILE, C), jnp.bfloat16),
                pltpu.SemaphoreType.DMA((n,)),
            ]
        return pl.pallas_call(
            lambda *refs: update_kernel(*refs, count=len(backs), first=first),
            grid_spec=pltpu.PrefetchScalarGridSpec(
                num_scalar_prefetch=2,
                grid=(tile_count,),
                in_specs=[by_tile, row] + [ANY] * len(backs) + ([] if first else [row]),
                out_specs=out_specs,
                scratch_shapes=scratch,
            ),
            out_shape=out_shape,
            compiler_params=pltpu.CompilerParams(vmem_limit_bytes=VMEM),
            name="update",
        )(owners, mine, gathered, class_rows, *backs, *([] if first else [state]))

    def exchange(array):
        return lax.all_to_all(array, "shard", split_axis=0, concat_axis=0, tiled=True)

    kernels = gathered = None
    pushes = []
    for b, slots in enumerate(batches):
        kernels, gathered, *done = batch_call(b, [flying[k] for k in slots], kernels, gathered)
        pushes += done
    for k in range(slot_count):
        out = pushes[k].astype(jnp.float16)
        ahead = slot_count + k - FLIGHT if k >= FLIGHT else min(HOLD + k, slot_count - 1)
        out, flying[ahead] = lax.optimization_barrier((out, flying[ahead]))
        flying.append(swap(out, k))
    backs = [back.astype(jnp.float32) for back in flying[slot_count:]]
    shares, labels, send = update_call(mine_x, gathered, backs, None)

    incoming = exchange(send)
    rounded = labels.astype(jnp.bfloat16)
    pushes = push_call(kernels, rounded)
    pushes, incoming = lax.optimization_barrier((pushes.astype(jnp.float16), incoming))
    back = exchange(pushes).astype(jnp.float32)
    gathered = gather_call(kernels, incoming, labels)
    owners = jnp.where(shard_ids == me, -1, mine)
    (labels,) = update_call(owners, gathered, [back], shares)
    return labels.reshape(embed.shape[0], C)


def solution(mesh):
    in_specs = (
        P(("groups", "shard"), None),
        P(("groups", "shard")),
        P(("groups", "shard")),
        P(("groups", "shard"), None),
        P(("groups", "shard")),
        P(("groups", "shard")),
    )
    out_specs = P(("groups", "shard"), None)
    return jax.shard_map(body, mesh=mesh, in_specs=in_specs, out_specs=out_specs, check_vma=False)
```

```python
import math

import jax
import jax.numpy as jnp
from jax import lax
from jax.experimental import pallas as pl
from jax.experimental.pallas import tpu as pltpu
from jax.sharding import PartitionSpec as P

C = 256
TILE = 256
ITERS = 2
WINDOW = 8
FIRST = 2
AFTER = 3
FLIGHT = 8
HOLD = 11
BATCH = 4
VMEM = 40 * 1024 * 1024

sharpness = 1.0
mixing = 0.8

LOG2E = math.log2(math.e)
ANY = pl.BlockSpec(memory_space=pl.ANY)

PEER, MINE, COUNT, LIST = 0, 1, 2, 3


def take_kernel(mine, me, src, *rest, peers):
    size = len(peers)
    outs, stage, arrive, leave = rest[:size], rest[size], rest[size + 1], rest[size + 2]
    loads = [
        pltpu.make_async_copy(src.at[mine[me[0] ^ peer]], stage.at[k], arrive.at[k])
        for k, peer in enumerate(peers)
    ]
    stores = [pltpu.make_async_copy(stage.at[k], out, leave.at[k]) for k, out in enumerate(outs)]
    for load in loads:
        load.start()
    for load, store in zip(loads, stores):
        load.wait()
        store.start()
    for store in stores:
        store.wait()


def batch_kernel(table, tiles, bias, meta, own, *rest, slots, begun, scale):
    size = len(slots)
    erem, lrem = rest[:size], rest[size : 2 * size]
    kout, gout, pouts = rest[-2 - size], rest[-1 - size], rest[-size:]
    gout[...] = rest[2 * size][...] if begun else own[...].astype(jnp.float32)
    for k, slot in enumerate(slots):
        pouts[k][...] = jnp.zeros_like(pouts[k])
        row = meta[table[slot, PEER]][:1]

        def pair(g, carry, k=k, slot=slot, row=row):
            tile = table[slot, LIST + g]
            inner = lax.dot_general(
                tiles[tile], erem[k][...], (((1,), (1,)), ((), ())), preferred_element_type=jnp.float32
            )
            kernel = jnp.exp2(inner * scale + (bias[tile] + row)).astype(jnp.bfloat16)
            kout[k * tiles.shape[0] + g] = kernel
            gout[tile] += jnp.dot(kernel, lrem[k][0], preferred_element_type=jnp.float32)
            pouts[k][...] += lax.dot_general(
                kernel, own[tile], (((0,), (0,)), ((), ())), preferred_element_type=jnp.float32
            )
            return carry

        lax.fori_loop(0, table[slot, COUNT], pair, 0)


def push_kernel(table, kref, own, pout):
    slot = pl.program_id(0)
    pout[...] = jnp.zeros_like(pout)

    def pair(g, carry):
        pout[0] += lax.dot_general(
            kref[g],
            own[table[slot, LIST + g]],
            (((0,), (0,)), ((), ())),
            preferred_element_type=jnp.float32,
        )
        return carry

    lax.fori_loop(0, table[slot, COUNT], pair, 0)


def gather_kernel(table, kref, lrem, labels, gout):
    slot = pl.program_id(0)

    @pl.when(slot == 0)
    def _():
        gout[...] = labels[...]

    def pair(g, carry):
        gout[table[slot, LIST + g]] += jnp.dot(kref[g], lrem[0], preferred_element_type=jnp.float32)
        return carry

    lax.fori_loop(0, table[slot, COUNT], pair, 0)


def update_kernel(owners, mine, gathered, classes, *rest, count, first):
    backs, rest = rest[:count], rest[count:]
    if first:
        shares, out, send, total, arrived, arrive, rounded, leave = rest
    else:
        shares, out, total, arrived, arrive = rest
    tile = pl.program_id(0)

    def load(k):
        source = backs[k] if first else backs[0].at[k]
        return pltpu.make_async_copy(source, arrived.at[k], arrive.at[k])

    def store(k):
        return pltpu.make_async_copy(rounded.at[mine[k]], send.at[k], leave.at[k])

    slots = range(owners.shape[0])

    @pl.when(tile == 0)
    def _():
        for k in slots:

            @pl.when(owners[k] >= 0)
            def _(k=k):
                load(k).start()

    total[...] = gathered[0]
    for k in slots:

        @pl.when(owners[k] == tile)
        def _(k=k):
            load(k).wait()
            total[...] += arrived[k]

    summed = total[...]
    diagonal = lax.broadcasted_iota(jnp.int32, (TILE, TILE), 0) == lax.broadcasted_iota(
        jnp.int32, (TILE, TILE), 1
    )
    ids = jnp.sum(jnp.where(diagonal, classes[0], 0.0), axis=1, keepdims=True)
    hot = ids == lax.broadcasted_iota(jnp.int32, (TILE, C), 1).astype(jnp.float32)
    if first:
        share = mixing / jnp.sum(summed, axis=1, keepdims=True)
        shares[0] = jnp.sum(jnp.where(diagonal, share, 0.0), axis=0, keepdims=True)
    else:
        share = jnp.sum(jnp.where(diagonal, shares[0], 0.0), axis=1, keepdims=True)
    blended = summed * share + jnp.where(hot, 1.0 - mixing, 0.0)
    squared = blended * blended
    labels = squared * (1.0 / jnp.sum(squared, axis=1, keepdims=True))
    out[0] = labels
    if first:
        rounded[tile] = labels.astype(jnp.bfloat16)
        for k in range(send.shape[0]):

            @pl.when(mine[k] == tile)
            def _(k=k):
                store(k).start()

        @pl.when(tile == pl.num_programs(0) - 1)
        def _():
            for k in range(send.shape[0]):
                store(k).wait()


def body(embed, seed_mask, seed_class, partner, pair_local, pair_peer):
    n = lax.axis_size("shard")
    me = lax.axis_index("shard")
    features = embed.shape[1]
    tiles = embed.reshape(-1, TILE, features)
    tile_count = tiles.shape[0]
    mine = partner.reshape(-1)
    half = n // 2
    order = []
    for k in range(half):
        order.append(half + k)
        if k + 1 < half:
            order.append(k + 1)
    slot_count = len(order)
    batches = [list(range(b, min(b + BATCH, slot_count))) for b in range(0, slot_count, BATCH)]

    tile_ids = jnp.arange(tile_count, dtype=jnp.int32)
    shard_ids = jnp.arange(n, dtype=jnp.int32)
    peers = jnp.array(order, jnp.int32) ^ me
    mine_x = jnp.sum(jnp.where(peers[:, None] == shard_ids[None, :], mine[None, :], 0), axis=1)
    sends = jnp.stack([peers, mine_x], axis=1).astype(jnp.int32)
    active = jnp.any(
        (pair_peer[None, None, :] == peers[:, None, None])
        & (pair_local[None, None, :] == tile_ids[None, :, None]),
        axis=2,
    )
    counts = jnp.sum(active.astype(jnp.int32), axis=1)
    place = jnp.sum(
        (active[:, None, :] & (tile_ids[None, None, :] < tile_ids[None, :, None])).astype(jnp.int32), axis=2
    )
    listed = jnp.sum(
        jnp.where(
            active[:, None, :] & (place[:, None, :] == tile_ids[None, :, None]), tile_ids[None, None, :], 0
        ),
        axis=2,
    )
    table = jnp.concatenate([sends, counts[:, None], listed], axis=1).astype(jnp.int32)

    def swap(value, k):
        return lax.ppermute(value, "shard", [(q, q ^ order[k]) for q in range(n)])

    def take(slots):
        size = len(slots)
        return pl.pallas_call(
            lambda *refs: take_kernel(*refs, peers=[order[k] for k in slots]),
            grid_spec=pltpu.PrefetchScalarGridSpec(
                num_scalar_prefetch=2,
                grid=(1,),
                in_specs=[ANY],
                out_specs=[ANY] * size,
                scratch_shapes=[
                    pltpu.VMEM((size, TILE, features), embed.dtype),
                    pltpu.SemaphoreType.DMA((size,)),
                    pltpu.SemaphoreType.DMA((size,)),
                ],
            ),
            out_shape=[jax.ShapeDtypeStruct((TILE, features), embed.dtype)] * size,
            name="take",
        )(mine, me.reshape(1), tiles)

    outgoing = list(take(list(range(FIRST)))) + list(take(list(range(FIRST, slot_count))))
    flying = []
    for k in range(slot_count):
        out = outgoing[k]
        if k >= WINDOW:
            out, flying[k - WINDOW] = lax.optimization_barrier((out, flying[k - WINDOW]))
        flying.append(swap(out, k))

    norms = jnp.sum(jnp.square(tiles.astype(jnp.float32)), axis=2)
    bias = (1.0 - norms * (1.0 / features)) * (sharpness * LOG2E)
    classes = jnp.where(seed_mask == 1, seed_class, -1).reshape(tile_count, TILE).astype(jnp.float32)
    meta = jnp.stack([bias, classes], axis=1)
    meta_out, flying[AFTER] = lax.optimization_barrier((meta[mine], flying[AFTER]))
    meta_in = lax.all_to_all(meta_out, "shard", split_axis=0, concat_axis=0, tiled=True)
    class_ids = jnp.arange(C, dtype=jnp.float32)

    def first_labels(ids):
        hot = (ids[..., None] == class_ids).astype(jnp.float32)
        return jnp.where(ids[..., None] < 0, 1.0 / C, hot).astype(jnp.bfloat16)

    own = first_labels(classes)
    own_in = first_labels(meta_in[:, 1])
    bias_column = bias[:, :, None]
    class_rows = classes[:, None, :]

    block = (1, TILE, C)
    store = (tile_count, TILE, TILE)
    sums = jax.ShapeDtypeStruct((TILE, C), jnp.float32)
    all_sums = jax.ShapeDtypeStruct((n, TILE, C), jnp.float32)
    tile_sums = jax.ShapeDtypeStruct((tile_count, TILE, C), jnp.float32)
    kernel_store = jax.ShapeDtypeStruct((len(batches) * BATCH * tile_count, TILE, TILE), jnp.bfloat16)

    def full(array):
        return pl.BlockSpec(array.shape, lambda g, t: (0,) * len(array.shape))

    def by_peer(slot):
        return pl.BlockSpec(block, lambda g, t: (t[slot, PEER], 0, 0))

    def batch_call(index, erem, kernels, gathered):
        slots = batches[index]
        size = len(slots)
        args = [tiles, bias_column, meta_in, own] + erem + [own_in] * size
        in_specs = [full(a) for a in args[: 4 + size]] + [by_peer(s) for s in slots]
        aliases = {}
        if index:
            args += [gathered, kernels]
            in_specs += [full(tile_sums), ANY]
            aliases = {len(args): 0}
        return pl.pallas_call(
            lambda *refs: batch_kernel(
                *refs, slots=slots, begun=index > 0, scale=2.0 * sharpness * LOG2E / features
            ),
            grid_spec=pltpu.PrefetchScalarGridSpec(
                num_scalar_prefetch=1,
                grid=(1,),
                in_specs=in_specs,
                out_specs=[
                    pl.BlockSpec((BATCH * tile_count, TILE, TILE), lambda g, t: (index, 0, 0)),
                    full(tile_sums),
                ]
                + [full(sums)] * size,
            ),
            out_shape=[kernel_store, tile_sums] + [sums] * size,
            input_output_aliases=aliases,
            compiler_params=pltpu.CompilerParams(vmem_limit_bytes=VMEM),
            cost_estimate=pl.CostEstimate(flops=int(1e10), bytes_accessed=int(3e7), transcendentals=0),
            name="batch",
        )(table, *args)

    def push_call(kernels, own):
        return pl.pallas_call(
            push_kernel,
            grid_spec=pltpu.PrefetchScalarGridSpec(
                num_scalar_prefetch=1,
                grid=(slot_count,),
                in_specs=[pl.BlockSpec(store, lambda g, t: (g, 0, 0)), full(own)],
                out_specs=pl.BlockSpec(block, lambda g, t: (t[g, PEER], 0, 0)),
            ),
            out_shape=all_sums,
            compiler_params=pltpu.CompilerParams(vmem_limit_bytes=VMEM),
            cost_estimate=pl.CostEstimate(flops=int(2e10), bytes_accessed=int(6e7), transcendentals=0),
            name="push",
        )(table, kernels, own)

    def gather_call(kernels, incoming, labels):
        return pl.pallas_call(
            gather_kernel,
            grid_spec=pltpu.PrefetchScalarGridSpec(
                num_scalar_prefetch=1,
                grid=(slot_count,),
                in_specs=[
                    pl.BlockSpec(store, lambda g, t: (g, 0, 0)),
                    pl.BlockSpec(block, lambda g, t: (t[g, PEER], 0, 0)),
                    full(labels),
                ],
                out_specs=full(tile_sums),
            ),
            out_shape=tile_sums,
            compiler_params=pltpu.CompilerParams(vmem_limit_bytes=VMEM),
            cost_estimate=pl.CostEstimate(flops=int(2e10), bytes_accessed=int(6e7), transcendentals=0),
            name="gather",
        )(table, kernels, incoming, labels)

    def update_call(owners, gathered, backs, state):
        first = state is None
        by_tile = pl.BlockSpec(block, lambda g, o, m: (g, 0, 0))
        row = pl.BlockSpec((1, 1, TILE), lambda g, o, m: (g, 0, 0))
        out_shape, out_specs = [tile_sums], [by_tile]
        slots = owners.shape[0]
        scratch = [
            pltpu.VMEM((TILE, C), jnp.float32),
            pltpu.VMEM((slots, TILE, C), jnp.float32),
            pltpu.SemaphoreType.DMA((slots,)),
        ]
        if first:
            row_shape = jax.ShapeDtypeStruct((tile_count, 1, TILE), jnp.float32)
            out_shape = [row_shape, tile_sums, pltpu.HBM((n, TILE, C), jnp.bfloat16)]
            out_specs = [row, by_tile, pl.BlockSpec(memory_space=pltpu.HBM)]
            scratch += [
                pltpu.VMEM((tile_count, TILE, C), jnp.bfloat16),
                pltpu.SemaphoreType.DMA((n,)),
            ]
        return pl.pallas_call(
            lambda *refs: update_kernel(*refs, count=len(backs), first=first),
            grid_spec=pltpu.PrefetchScalarGridSpec(
                num_scalar_prefetch=2,
                grid=(tile_count,),
                in_specs=[by_tile, row] + [ANY] * len(backs) + ([] if first else [row]),
                out_specs=out_specs,
                scratch_shapes=scratch,
            ),
            out_shape=out_shape,
            compiler_params=pltpu.CompilerParams(vmem_limit_bytes=VMEM),
            name="update",
        )(owners, mine, gathered, class_rows, *backs, *([] if first else [state]))

    def exchange(array):
        return lax.all_to_all(array, "shard", split_axis=0, concat_axis=0, tiled=True)

    kernels = gathered = None
    pushes = []
    for b, slots in enumerate(batches):
        kernels, gathered, *done = batch_call(b, [flying[k] for k in slots], kernels, gathered)
        pushes += done
    for k in range(slot_count):
        out = pushes[k].astype(jnp.float16)
        ahead = slot_count + k - FLIGHT if k >= FLIGHT else min(HOLD + k, slot_count - 1)
        out, flying[ahead] = lax.optimization_barrier((out, flying[ahead]))
        flying.append(swap(out, k))
    backs = [back.astype(jnp.float32) for back in flying[slot_count:]]
    shares, labels, send = update_call(mine_x, gathered, backs, None)

    incoming = exchange(send)
    rounded = labels.astype(jnp.bfloat16)
    pushes = push_call(kernels, rounded)
    pushes, incoming = lax.optimization_barrier((pushes.astype(jnp.float16), incoming))
    back = exchange(pushes).astype(jnp.float32)
    gathered = gather_call(kernels, incoming, labels)
    owners = jnp.where(shard_ids == me, -1, mine)
    (labels,) = update_call(owners, gathered, [back], shares)
    return labels.reshape(embed.shape[0], C)


def solution(mesh):
    in_specs = (
        P(("groups", "shard"), None),
        P(("groups", "shard")),
        P(("groups", "shard")),
        P(("groups", "shard"), None),
        P(("groups", "shard")),
        P(("groups", "shard")),
    )
    out_specs = P(("groups", "shard"), None)
    return jax.shard_map(body, mesh=mesh, in_specs=in_specs, out_specs=out_specs, check_vma=False)
```
